32 devices in a mesh: rep: 2 (over x), patch: 8 (over z, y), grp: 2 (over core).
Axes of the slice: x: 2, y: 2, z: 4, core: 2. Of those that a mesh axis runs over, the one named last changes fastest.
Arguments:
- queries: bfloat16 [2560, 1536], P(('rep', 'patch', 'grp')), parts along dimension 0, may hold values from -6 to 6
- keys: bfloat16 [2560, 1536], P(('rep', 'patch', 'grp')), parts along dimension 0, may hold values from -6 to 6
- values: bfloat16 [2560, 1536], P(('rep', 'patch', 'grp')), parts along dimension 0, may hold values from -6 to 6
- stale_keys: bfloat16 [2560, 1536], P(('rep', 'patch', 'grp')), parts along dimension 0, may hold values from -4 to 4
- stale_values: bfloat16 [2560, 1536], P(('rep', 'patch', 'grp')), parts along dimension 0, may hold values from -6 to 6
- q_gain: float32 [128], replicated, may hold values from 1 to 3
- k_gain: float32 [128], replicated, may hold values from 1 to 3
- o_weight: bfloat16 [1536, 3072], replicated, may hold values from -0.15625 to 0.15625
- slot_positions: int32 [2560], P('rep'), parts along dimension 0, may hold values from 0 to 1279, each once
Outputs:
- attended: bfloat16 [2560, 3072], P(('rep', 'patch', 'grp')), parts along dimension 0
The draws below stay inside these ranges and needn't reach their ends.
There are 2 independent parts, one for each index of `rep`. The reference program is written for one: setup_inputs(seed, part) draws one part's arguments, and reference() takes and returns one part's arrays. A program takes and returns all parts, laid end to end along the dimension named above; an argument that names none is the same for every part. Nothing has to cross between parts.
Inputs may be any that keep to these rules, and one draw needn't show every extreme that they name: `slot_positions`: a permutation of the slots' patch positions; positions 1275 and above mark padding.
All inputs are finite; a program needn't handle non-finite values.
Results may differ from the reference program's by a relative error of at most 0.012.
Values may be sent and summed in bfloat16 or wider, within the bound.
A program may use at most 192 MiB of HBM per device.

```python
import math
import jax
import jax.numpy as jnp
from jax import lax

D = 3072
HEADS = 12
HEAD_DIM = 128
LAT_H = 34
LAT_W = 60
TOK_DEV = 80
SEQ = 1280
VALID = 1275


def draw_stale_keys(key, part):
    key = jax.random.fold_in(key, 11)
    radius_key, phase_key = jax.random.split(key)
    half_dim = HEAD_DIM // 2
    radius = jnp.exp(jax.random.uniform(radius_key, (1, HEADS, half_dim), jnp.float32, 0.0, math.log(3.0)))
    phase = jax.random.uniform(phase_key, (SEQ, HEADS, half_dim), jnp.float32, -math.pi, math.pi)
    first_part = radius * jnp.cos(phase)
    second_part = radius * jnp.sin(phase)
    pieces_out = []
    offset_at = 0
    for width in (HEAD_DIM // 8, 7 * HEAD_DIM // 16, 7 * HEAD_DIM // 16):
        half_width = width // 2
        pieces_out.append(first_part[..., offset_at:offset_at + half_width])
        pieces_out.append(second_part[..., offset_at:offset_at + half_width])
        offset_at = offset_at + half_width
    joined = jnp.concatenate(pieces_out, axis=-1)
    return joined.reshape(SEQ, HEADS * HEAD_DIM).astype(jnp.bfloat16)


def levels(own_key, extent, shards, low, high):
    level = 1.0
    for axis_at, parts in shards:
        steps = jax.random.uniform(jax.random.fold_in(jax.random.fold_in(own_key, 6), axis_at), (parts,), jnp.float32, low / len(shards), high / len(shards))
        level = level * jnp.repeat(jnp.exp(steps), extent[axis_at] // parts).reshape((-1,) + (1,) * (len(extent) - 1 - axis_at))
    return level


def centred(key, dims, spread, most, pieces=(), held_as=jnp.bfloat16):
    values = jax.random.normal(key, dims, jnp.float32) * spread
    if len(pieces) > 0:
        values = levels(key, dims, pieces, -0.22, 0.18) * values
    return jnp.clip(values, min=-most, max=most).astype(held_as)


def setup_inputs(seed: int = 0, part: int = 0) -> dict:
    splits = jax.random.split(jax.random.key(seed), 10)
    own_keys = jax.random.split(jax.random.fold_in(splits[9], part), 10)
    queries = centred(own_keys[0], (SEQ, HEADS * HEAD_DIM), 1.0, 6.0, ((0, 16),))
    keys = centred(own_keys[1], (SEQ, HEADS * HEAD_DIM), 1.0, 6.0, ((0, 16),))
    values = centred(own_keys[2], (SEQ, HEADS * HEAD_DIM), 1.0, 6.0, ((0, 16),))
    stale_keys = draw_stale_keys(jax.random.fold_in(jax.random.fold_in(splits[9], part), 71), part)
    stale_values = centred(own_keys[4], (SEQ, HEADS * HEAD_DIM), 1.0, 6.0, ((0, 16),))
    q_gain = jnp.clip(jnp.exp(jax.random.uniform(splits[5], (HEAD_DIM,), jnp.float32, math.log(1.0), math.log(3.0))), 1.0, 3.0)
    k_gain = jnp.clip(jnp.exp(jax.random.uniform(splits[6], (HEAD_DIM,), jnp.float32, math.log(1.0), math.log(3.0))), 1.0, 3.0)
    o_weight = centred(splits[7], (HEADS * HEAD_DIM, D), (HEADS * HEAD_DIM) ** -0.5, 0.15625)
    slot_positions = jax.random.permutation(own_keys[8], SEQ).astype(jnp.int32)
    return dict(queries=queries, keys=keys, values=values, stale_keys=stale_keys, stale_values=stale_values, q_gain=q_gain, k_gain=k_gain, o_weight=o_weight, slot_positions=slot_positions)


def rotary(rows_f, pos_ids):
    head_dim = rows_f.shape[-1]
    per_frame = LAT_H * LAT_W
    frame_pos = (pos_ids // per_frame).astype(jnp.float32)
    row_pos = (pos_ids // LAT_W % LAT_H).astype(jnp.float32)
    col_pos = (pos_ids % LAT_W).astype(jnp.float32)
    pieces_out = []
    offset_at = 0
    for coord_pos, width in ((frame_pos, head_dim // 8), (row_pos, 7 * head_dim // 16), (col_pos, 7 * head_dim // 16)):
        half_width = width // 2
        frequency = 256.0 ** (-jnp.arange(half_width, dtype=jnp.float32) * 2.0 / width)
        angles = coord_pos[:, None] * frequency[None, :]
        cosine = jnp.cos(angles)[:, None, :]
        sine = jnp.sin(angles)[:, None, :]
        first_half = rows_f[..., offset_at:offset_at + half_width]
        second_half = rows_f[..., offset_at + half_width:offset_at + width]
        pieces_out.append(first_half * cosine - second_half * sine)
        pieces_out.append(first_half * sine + second_half * cosine)
        offset_at = offset_at + width
    return jnp.concatenate(pieces_out, axis=-1)

def prepare(projected, gain, pos_ids):
    row_count = projected.shape[0]
    head_dim = gain.shape[0]
    rows_f = projected.astype(jnp.float32).reshape(row_count, -1, head_dim)
    mean_sq = lax.optimization_barrier(jnp.mean(rows_f * rows_f, axis=-1, keepdims=True))
    normed = rows_f * lax.rsqrt(mean_sq + 1e-06) * gain
    return rotary(normed, pos_ids).astype(jnp.bfloat16)

def reference(queries, keys, values, stale_keys, stale_values, q_gain, k_gain, o_weight, slot_positions):
    seq_len = queries.shape[0]
    head_dim = q_gain.shape[0]
    head_count = queries.shape[1] // head_dim
    q_rot = prepare(queries, q_gain, slot_positions)
    k_rot = prepare(keys, k_gain, slot_positions)
    fresh_v = values.reshape(seq_len, head_count, head_dim)
    old_k = stale_keys.reshape(seq_len, head_count, head_dim)
    old_v = stale_values.reshape(seq_len, head_count, head_dim)
    subgroup = jnp.arange(seq_len, dtype=jnp.int32) // TOK_DEV % 2
    live = slot_positions < VALID
    inv_root = 1.0 / head_dim ** 0.5

    def one_head(head_idx):
        q_head = q_rot[:, head_idx]
        results = []
        for side_idx in (0, 1):
            same = (subgroup == side_idx)[:, None]
            key_set = jnp.where(same, k_rot[:, head_idx], old_k[:, head_idx])
            value_set = jnp.where(same, fresh_v[:, head_idx], old_v[:, head_idx])
            scores = jnp.dot(q_head, key_set.T, preferred_element_type=jnp.float32) * inv_root
            scores = jnp.where(live[None, :], scores, -1e+30)
            top = lax.optimization_barrier(jnp.max(scores, axis=1, keepdims=True))
            probs = jnp.exp(scores - top)
            total = lax.optimization_barrier(jnp.sum(probs, axis=1))
            summed = jnp.dot(probs.astype(jnp.bfloat16), value_set, preferred_element_type=jnp.float32)
            results.append(summed / total[:, None])
        return jnp.where((subgroup == 0)[:, None], results[0], results[1])
    per_head = lax.map(one_head, jnp.arange(head_count, dtype=jnp.int32))
    attn = per_head.transpose(1, 0, 2).reshape(seq_len, head_count * head_dim).astype(jnp.bfloat16)
    projected = jnp.dot(attn, o_weight, preferred_element_type=jnp.float32)
    return jnp.where(live[:, None], projected, 0.0).astype(jnp.bfloat16)
```

```python
import functools

import jax
import jax.numpy as jnp
import numpy as np
from jax import lax
from jax.experimental import pallas as pl
from jax.experimental.pallas import tpu as pltpu
from jax.sharding import PartitionSpec as P

LAT_H = 34
LAT_W = 60
GROUPS = 4
MESH = pl.DeviceIdType.MESH


def swap_lanes(head_dim):
    order = []
    at = 0
    for width in (head_dim // 8, 7 * head_dim // 16, 7 * head_dim // 16):
        half = width // 2
        order += list(range(at + half, at + width)) + list(range(at, at + half))
        at += width
    return np.array(order)


def tables(pos_ids, head_dim):
    per_frame = LAT_H * LAT_W
    coords = (pos_ids // per_frame, pos_ids // LAT_W % LAT_H, pos_ids % LAT_W)
    freq = []
    which = []
    sign = []
    for idx, width in enumerate((head_dim // 8, 7 * head_dim // 16, 7 * head_dim // 16)):
        half = width // 2
        f = np.float32(256.0) ** (-np.arange(half, dtype=np.float32) * np.float32(2.0) / np.float32(width))
        freq += list(f) + list(f)
        which += [idx] * width
        sign += [-1.0] * half + [1.0] * half
    freq = jnp.asarray(np.array(freq, np.float32))[None, :]
    which = np.array(which)[None, :]
    sign = jnp.asarray(np.array(sign, np.float32))[None, :]
    f_pos, r_pos, c_pos = (x.astype(jnp.float32)[:, None] for x in coords)
    coord = jnp.where(which == 0, f_pos, jnp.where(which == 1, r_pos, c_pos))
    angles = coord * freq
    return jnp.cos(angles), jnp.sin(angles) * sign


def kernel(
    n_patch, heads, head_dim, rows,
    q_ref, k_ref, v_ref, sk_ref, sv_ref, tab_ref, perm_ref, bias_ref,
    out_ref,
    qrot, krot, qbuf, kv, osend, obuf,
    q_ssem, kv_ssem, f_ssem, o_ssem, q_rsem, kv_rsem, o_rsem,
):
    rep = lax.axis_index("rep")
    p = lax.axis_index("patch")
    c = lax.axis_index("grp")
    hpg = heads // GROUPS
    width = hpg * head_dim
    per_group = n_patch // GROUPS
    n_chunk = per_group // 2
    chunk = n_patch // n_chunk
    per_core = chunk // 2
    my_hg = p // per_group
    my_s = p % 2
    my_qc = (p % per_group) // 2

    barrier = pltpu.get_barrier_semaphore()
    n_dev = 2 * n_patch

    def greet(i, carry):
        other = lax.rem(p * 2 + c + i, n_dev)
        pl.semaphore_signal(
            barrier, inc=1, device_id=(rep, other // 2, other % 2), device_id_type=MESH
        )
        return carry

    lax.fori_loop(1, n_dev, greet, 0)
    pl.semaphore_wait(barrier, n_dev - 1)

    pending = []

    def send(src, dst, ssem, rsem, dp, dc):
        away = jnp.logical_or(dp != p, dc != c)
        remote = pltpu.make_async_remote_copy(
            src_ref=src, dst_ref=dst, send_sem=ssem, recv_sem=rsem,
            device_id=(rep, dp, dc), device_id_type=MESH,
        )

        @pl.when(away)
        def _():
            remote.start()

        @pl.when(jnp.logical_not(away))
        def _():
            pltpu.make_async_copy(src, dst, rsem).start()

        pending.append((away, remote))

    def row_slice(i):
        return pl.ds(pl.multiple_of(i * rows, 16), rows)

    def col_slice(g):
        return pl.ds(pl.multiple_of(g * width, 128), width)

    def send_kv(kind, ref):
        stale = kind < 2
        s = (1 - c) if stale else c
        for step in range(GROUPS):
            g = lax.rem(my_hg + 1 + step, GROUPS)
            for qc in range(n_chunk):
                dp = g * per_group + qc * 2 + s
                send(
                    ref.at[:, col_slice(g)], kv.at[kind, row_slice(p), :],
                    kv_ssem.at[kind, step * n_chunk + qc], kv_rsem.at[kind, p], dp, p % 2,
                )

    def prepare(ref, which, dst):
        a = tab_ref[2 * which]
        b = tab_ref[2 * which + 1]
        for h in range(heads):
            cols = slice(h * head_dim, (h + 1) * head_dim)
            xb = ref[:, cols]
            x = xb.astype(jnp.float32)
            xs = jnp.dot(xb, perm_ref[...], preferred_element_type=jnp.float32)
            mean_sq = jnp.mean(x * x, axis=-1, keepdims=True)
            dst[:, cols] = ((x * a + xs * b) * lax.rsqrt(mean_sq + 1e-06)).astype(jnp.bfloat16)

    send_kv(0, sk_ref)
    send_kv(1, sv_ref)
    prepare(q_ref, 0, qrot)
    for step in range(GROUPS):
        g = lax.rem(my_hg + 1 + step, GROUPS)
        dp = g * per_group + (p // chunk) * 2 + c
        dc = (p % chunk) // per_core
        slot = p % per_core
        send(
            qrot.at[:, col_slice(g)], qbuf.at[row_slice(slot), :],
            q_ssem.at[step], q_rsem.at[slot], dp, dc,
        )
    prepare(k_ref, 1, krot)
    send_kv(2, krot)
    send_kv(3, v_ref)

    def kv_wait(kind, src):
        piece = kv.at[kind, row_slice(src), :]
        pltpu.make_async_copy(piece, piece, kv_rsem.at[kind, src]).wait()

    def forward(kind, i):
        src = 2 * i + c
        kv_wait(kind, src)
        piece = kv.at[kind, row_slice(src), :]
        copy = pltpu.make_async_remote_copy(
            src_ref=piece, dst_ref=piece,
            send_sem=f_ssem.at[kind, i], recv_sem=kv_rsem.at[kind, src],
            device_id=(rep, p, 1 - c), device_id_type=MESH,
        )
        copy.start()
        return copy

    forwards = []
    n_q = per_core * rows
    state = [None] * hpg
    inv_root = 1.0 / head_dim**0.5
    blk = chunk * rows
    for part in range(2):
        for i in range(n_patch // 2):
            forwards.append(forward(2 * part, i))
            forwards.append(forward(2 * part + 1, i))
        if part == 0:
            for slot in range(per_core):
                piece = qbuf.at[row_slice(slot), :]
                pltpu.make_async_copy(piece, piece, q_rsem.at[slot]).wait()
        for i in range(n_patch // 2):
            kv_wait(2 * part, 2 * i + (1 - c))
            kv_wait(2 * part + 1, 2 * i + (1 - c))
        side = (1 - my_s) if part == 0 else my_s
        for at in range(0, n_patch * rows, blk):
            bias = bias_ref[pl.ds(side, 1), at : at + blk]
            for h in range(hpg):
                cols = slice(h * head_dim, (h + 1) * head_dim)
                scores = lax.dot_general(
                    qbuf[:, cols], kv[2 * part, at : at + blk, cols],
                    (((1,), (1,)), ((), ())), preferred_element_type=jnp.float32,
                )
                scores = scores * inv_root + bias
                top = jnp.max(scores, axis=1, keepdims=True)
                if state[h] is not None:
                    top = jnp.maximum(top, state[h][0])
                probs = jnp.exp(scores - top)
                total = jnp.sum(probs, axis=1, keepdims=True)
                acc = jnp.dot(
                    probs.astype(jnp.bfloat16), kv[2 * part + 1, at : at + blk, cols],
                    preferred_element_type=jnp.float32,
                )
                if state[h] is not None:
                    fade = jnp.exp(state[h][0] - top)
                    total = total + state[h][1] * fade
                    acc = acc + state[h][2] * fade
                state[h] = (top, total, acc)
    for h in range(hpg):
        cols = slice(h * head_dim, (h + 1) * head_dim)
        osend[:, cols] = (state[h][2] / state[h][1]).astype(jnp.bfloat16)
    for slot in range(per_core):
        dp = my_qc * chunk + c * per_core + slot
        send(
            osend.at[row_slice(slot), :], obuf.at[my_hg],
            o_ssem.at[slot], o_rsem.at[my_hg], dp, my_s,
        )
    for g in range(GROUPS):
        piece = obuf.at[g]
        pltpu.make_async_copy(piece, piece, o_rsem.at[g]).wait()
        out_ref[:, g * width : (g + 1) * width] = obuf[g]
    for copy in forwards:
        copy.wait_send()
    for away, remote in pending:

        @pl.when(away)
        def _():
            remote.wait_send()


def body(n_patch, queries, keys, values, stale_keys, stale_values, q_gain, k_gain, o_weight, slot_positions):
    rows = queries.shape[0]
    head_dim = q_gain.shape[0]
    heads = queries.shape[1] // head_dim
    seq_len = slot_positions.shape[0]
    live_count = seq_len - max(seq_len // 256, 2)
    my_block = lax.axis_index("patch") * 2 + lax.axis_index("grp")
    own_pos = lax.dynamic_slice_in_dim(slot_positions, my_block * rows, rows)
    cosine, sine = tables(own_pos, head_dim)
    order = swap_lanes(head_dim)
    tab = jnp.stack(
        [cosine * q_gain, sine * q_gain[order], cosine * k_gain, sine * k_gain[order]]
    )
    perm = np.zeros((head_dim, head_dim), np.float32)
    perm[order, np.arange(head_dim)] = 1.0
    perm = jnp.asarray(perm, jnp.bfloat16)
    bias = jnp.where(slot_positions < live_count, 0.0, -1e30).astype(jnp.float32)
    bias = bias.reshape(n_patch, 2, rows).transpose(1, 0, 2).reshape(2, n_patch * rows)
    width = heads // GROUPS * head_dim
    n_chunk = n_patch // GROUPS // 2
    per_core = n_patch // n_chunk // 2
    vmem = pl.BlockSpec(memory_space=pltpu.VMEM)
    attn = pl.pallas_call(
        functools.partial(kernel, n_patch, heads, head_dim, rows),
        out_shape=jax.ShapeDtypeStruct(queries.shape, jnp.bfloat16),
        in_specs=[vmem] * 8,
        out_specs=vmem,
        scratch_shapes=[
            pltpu.VMEM(queries.shape, jnp.bfloat16),
            pltpu.VMEM(queries.shape, jnp.bfloat16),
            pltpu.VMEM((per_core * rows, width), jnp.bfloat16),
            pltpu.VMEM((4, n_patch * rows, width), jnp.bfloat16),
            pltpu.VMEM((per_core * rows, width), jnp.bfloat16),
            pltpu.VMEM((GROUPS, rows, width), jnp.bfloat16),
            pltpu.SemaphoreType.DMA((GROUPS,)),
            pltpu.SemaphoreType.DMA((4, GROUPS * n_chunk)),
            pltpu.SemaphoreType.DMA((4, n_patch // 2)),
            pltpu.SemaphoreType.DMA((per_core,)),
            pltpu.SemaphoreType.DMA((per_core,)),
            pltpu.SemaphoreType.DMA((4, n_patch)),
            pltpu.SemaphoreType.DMA((GROUPS,)),
        ],
        compiler_params=pltpu.CompilerParams(
            collective_id=0, has_side_effects=True, vmem_limit_bytes=40 * 1024 * 1024
        ),
    )(queries, keys, values, stale_keys, stale_values, tab, perm, bias)
    projected = jnp.dot(attn, o_weight, preferred_element_type=jnp.float32)
    own_live = own_pos < live_count
    return jnp.where(own_live[:, None], projected, 0.0).astype(jnp.bfloat16)


def solution(mesh):
    split = P(("rep", "patch", "grp"), None)
    in_specs = (split, split, split, split, split, P(), P(), P(), P("rep"))
    return jax.shard_map(
        functools.partial(body, mesh.shape["patch"]),
        mesh=mesh, in_specs=in_specs, out_specs=split, check_vma=False,
    )
```

```python
import functools
import math

import jax
import jax.numpy as jnp
from jax import lax
from jax.experimental import pallas as pl
from jax.experimental.pallas import tpu as pltpu
from jax.sharding import PartitionSpec as P

LAT_H = 34
LAT_W = 60
GROUPS = 4
MESH = pl.DeviceIdType.MESH


def sections(head_dim):
    return (head_dim // 8, 7 * head_dim // 16, 7 * head_dim // 16)


def by_lane(lanes, head_dim, values):
    out = values[-1][2]
    for _, end, value in reversed(values[:-1]):
        out = jnp.where(lanes < end, value, out)
    return out


def rotary_tables(pos, head_dim):
    lanes = lax.broadcasted_iota(jnp.int32, (1, head_dim), 1)
    wide = lax.broadcasted_iota(jnp.int32, (head_dim, head_dim), 1)
    down = lax.broadcasted_iota(jnp.int32, (head_dim, head_dim), 0)
    line = jnp.floor((pos + 0.5) * (1.0 / LAT_W))
    col = pos - line * LAT_W
    frame = jnp.floor((line + 0.5) * (1.0 / LAT_H))
    row = line - frame * LAT_H
    at = 0
    starts, scales, signs, shifts, coords = [], [], [], [], []
    for width, coord in zip(sections(head_dim), (frame, row, col)):
        half = width // 2
        rate = -2.0 / width * math.log(256.0)
        for k in range(2):
            lo, hi = at + k * half, at + (k + 1) * half
            starts.append((lo, hi, float(lo)))
            scales.append((lo, hi, rate))
            signs.append((lo, hi, 1.0 if k else -1.0))
            shifts.append((lo, hi, -half if k else half))
        coords.append((at, at + width, coord))
        at += width
    step = lanes.astype(jnp.float32) - by_lane(lanes, head_dim, starts)
    freq = jnp.exp(step * by_lane(lanes, head_dim, scales))
    angles = by_lane(lanes, head_dim, coords) * freq
    swap = (down == wide + by_lane(wide, head_dim, shifts)).astype(jnp.float32)
    return jnp.cos(angles), jnp.sin(angles) * by_lane(lanes, head_dim, signs), swap


def row_to_column(row):
    n = row.shape[1]
    same = lax.broadcasted_iota(jnp.int32, (n, n), 0) == lax.broadcasted_iota(
        jnp.int32, (n, n), 1
    )
    return jnp.sum(jnp.where(same, row, 0.0), axis=1, keepdims=True)


def kernel(
    n_patch, heads, head_dim, rows,
    q_hbm, k_hbm, v_ref, sk_ref, sv_ref, qg_hbm, kg_hbm, w_hbm, pos_hbm,
    out_ref,
    q_ref, k_ref, qg_ref, kg_ref, w_ref, pos_ref,
    qrot, krot, qbuf, kv, osend, obuf,
    l_sem, q_ssem, kv_ssem, f_ssem, o_ssem, q_rsem, kv_rsem, o_rsem,
):
    rep = lax.axis_index("rep")
    p = lax.axis_index("patch")
    c = lax.axis_index("grp")
    hpg = heads // GROUPS
    width = hpg * head_dim
    per_group = n_patch // GROUPS
    n_chunk = per_group // 2
    chunk = n_patch // n_chunk
    per_core = chunk // 2
    my_hg = p // per_group
    my_s = p % 2
    my_qc = (p % per_group) // 2

    seq_len = 2 * n_patch * rows
    live_count = float(seq_len - max(seq_len // 256, 2))

    loads = [
        pltpu.make_async_copy(src, dst, l_sem.at[i])
        for i, (src, dst) in enumerate(
            (
                (pos_hbm, pos_ref), (qg_hbm, qg_ref), (kg_hbm, kg_ref),
                (q_hbm, q_ref), (k_hbm, k_ref), (w_hbm, w_ref),
            )
        )
    ]
    for load in loads[:5]:
        load.start()

    barrier = pltpu.get_barrier_semaphore()
    n_dev = 2 * n_patch

    def greet(i, carry):
        other = lax.rem(p * 2 + c + i, n_dev)
        pl.semaphore_signal(
            barrier, inc=1, device_id=(rep, other // 2, other % 2), device_id_type=MESH
        )
        return carry

    lax.fori_loop(1, n_dev, greet, 0)
    pl.semaphore_wait(barrier, n_dev - 1)

    pending = []

    def send(src, dst, ssem, rsem, dp, dc):
        away = jnp.logical_or(dp != p, dc != c)
        remote = pltpu.make_async_remote_copy(
            src_ref=src, dst_ref=dst, send_sem=ssem, recv_sem=rsem,
            device_id=(rep, dp, dc), device_id_type=MESH,
        )

        @pl.when(away)
        def _():
            remote.start()

        @pl.when(jnp.logical_not(away))
        def _():
            pltpu.make_async_copy(src, dst, rsem).start()

        pending.append((away, remote))

    def row_slice(i):
        return pl.ds(pl.multiple_of(i * rows, 16), rows)

    def col_slice(g):
        return pl.ds(pl.multiple_of(g * width, 128), width)

    def send_kv(kind, ref):
        stale = kind < 2
        s = (1 - c) if stale else c
        for step in range(GROUPS):
            g = lax.rem(my_hg + 1 + step, GROUPS)
            for qc in range(n_chunk):
                dp = g * per_group + qc * 2 + s
                send(
                    ref.at[:, col_slice(g)], kv.at[kind, row_slice(p), :],
                    kv_ssem.at[kind, step * n_chunk + qc], kv_rsem.at[kind, p], dp, p % 2,
                )

    def prepare(ref, gain_ref, dst):
        gain = gain_ref[...]
        a = cosine * gain
        b = sine * jnp.sum(swap * row_to_column(gain), axis=0, keepdims=True)
        for h in range(heads):
            cols = slice(h * head_dim, (h + 1) * head_dim)
            xb = ref[:, cols]
            x = xb.astype(jnp.float32)
            xs = jnp.dot(xb, swap_b, preferred_element_type=jnp.float32)
            mean_sq = jnp.mean(x * x, axis=-1, keepdims=True)
            dst[:, cols] = ((x * a + xs * b) * lax.rsqrt(mean_sq + 1e-06)).astype(jnp.bfloat16)

    send_kv(0, sk_ref)
    send_kv(1, sv_ref)
    loads[5].start()
    for load in loads[:5]:
        load.wait()
    pos = row_to_column(pos_ref[pl.ds(p * 2 + c, 1), :].astype(jnp.float32))
    cosine, sine, swap = rotary_tables(pos, head_dim)
    swap_b = swap.astype(jnp.bfloat16)
    prepare(q_ref, qg_ref, qrot)
    for step in range(GROUPS):
        g = lax.rem(my_hg + 1 + step, GROUPS)
        dp = g * per_group + (p // chunk) * 2 + c
        dc = (p % chunk) // per_core
        slot = p % per_core
        send(
            qrot.at[:, col_slice(g)], qbuf.at[row_slice(slot), :],
            q_ssem.at[step], q_rsem.at[slot], dp, dc,
        )
    prepare(k_ref, kg_ref, krot)
    send_kv(2, krot)
    send_kv(3, v_ref)

    def kv_wait(kind, src):
        piece = kv.at[kind, row_slice(src), :]
        pltpu.make_async_copy(piece, piece, kv_rsem.at[kind, src]).wait()

    def forward(kind, i):
        src = 2 * i + c
        kv_wait(kind, src)
        piece = kv.at[kind, row_slice(src), :]
        copy = pltpu.make_async_remote_copy(
            src_ref=piece, dst_ref=piece,
            send_sem=f_ssem.at[kind, i], recv_sem=kv_rsem.at[kind, src],
            device_id=(rep, p, 1 - c), device_id_type=MESH,
        )
        copy.start()
        return copy

    forwards = []
    n_q = per_core * rows
    state = [None] * hpg
    inv_root = 1.0 / head_dim**0.5
    blk = chunk * rows
    for part in range(2):
        for i in range(n_patch // 2):
            forwards.append(forward(2 * part, i))
            forwards.append(forward(2 * part + 1, i))
        if part == 0:
            for slot in range(per_core):
                piece = qbuf.at[row_slice(slot), :]
                pltpu.make_async_copy(piece, piece, q_rsem.at[slot]).wait()
        for i in range(n_patch // 2):
            kv_wait(2 * part, 2 * i + (1 - c))
            kv_wait(2 * part + 1, 2 * i + (1 - c))
        side = (1 - my_s) if part == 0 else my_s
        for at in range(0, n_patch * rows, blk):
            first = at // rows
            key_pos = jnp.concatenate(
                [pos_ref[pl.ds(2 * i + side, 1), :] for i in range(first, first + chunk)], axis=1
            )
            bias = jnp.where(key_pos.astype(jnp.float32) < live_count, 0.0, -1e30)
            for h in range(hpg):
                cols = slice(h * head_dim, (h + 1) * head_dim)
                scores = lax.dot_general(
                    qbuf[:, cols], kv[2 * part, at : at + blk, cols],
                    (((1,), (1,)), ((), ())), preferred_element_type=jnp.float32,
                )
                scores = scores * inv_root + bias
                top = jnp.max(scores, axis=1, keepdims=True)
                if state[h] is not None:
                    top = jnp.maximum(top, state[h][0])
                probs = jnp.exp(scores - top)
                total = jnp.sum(probs, axis=1, keepdims=True)
                acc = jnp.dot(
                    probs.astype(jnp.bfloat16), kv[2 * part + 1, at : at + blk, cols],
                    preferred_element_type=jnp.float32,
                )
                if state[h] is not None:
                    fade = jnp.exp(state[h][0] - top)
                    total = total + state[h][1] * fade
                    acc = acc + state[h][2] * fade
                state[h] = (top, total, acc)
    for h in range(hpg):
        cols = slice(h * head_dim, (h + 1) * head_dim)
        osend[:, cols] = (state[h][2] / state[h][1]).astype(jnp.bfloat16)
    for slot in range(per_core):
        dp = my_qc * chunk + c * per_core + slot
        send(
            osend.at[row_slice(slot), :], obuf.at[my_hg],
            o_ssem.at[slot], o_rsem.at[my_hg], dp, my_s,
        )
    for g in range(GROUPS):
        piece = obuf.at[g]
        pltpu.make_async_copy(piece, piece, o_rsem.at[g]).wait()
    attn = jnp.concatenate([obuf[g] for g in range(GROUPS)], axis=1)
    loads[5].wait()
    own_live = pos < live_count
    d_out = out_ref.shape[1]
    for at in range(0, d_out, 512):
        tile = jnp.dot(attn, w_ref[:, at : at + 512], preferred_element_type=jnp.float32)
        out_ref[:, at : at + 512] = jnp.where(own_live, tile, 0.0).astype(jnp.bfloat16)
    for copy in forwards:
        copy.wait_send()
    for away, remote in pending:

        @pl.when(away)
        def _():
            remote.wait_send()


def body(n_patch, queries, keys, values, stale_keys, stale_values, q_gain, k_gain, o_weight, slot_positions):
    rows = queries.shape[0]
    head_dim = q_gain.shape[0]
    heads = queries.shape[1] // head_dim
    width = heads // GROUPS * head_dim
    n_chunk = n_patch // GROUPS // 2
    per_core = n_patch // n_chunk // 2
    hbm = pl.BlockSpec(memory_space=pl.ANY)
    return pl.pallas_call(
        functools.partial(kernel, n_patch, heads, head_dim, rows),
        out_shape=jax.ShapeDtypeStruct((rows, o_weight.shape[1]), jnp.bfloat16),
        in_specs=[hbm] * 9,
        out_specs=pl.BlockSpec(memory_space=pltpu.VMEM),
        scratch_shapes=[
            pltpu.VMEM(queries.shape, jnp.bfloat16),
            pltpu.VMEM(queries.shape, jnp.bfloat16),
            pltpu.VMEM((1, head_dim), jnp.float32),
            pltpu.VMEM((1, head_dim), jnp.float32),
            pltpu.VMEM(o_weight.shape, jnp.bfloat16),
            pltpu.VMEM((2 * n_patch, rows), jnp.int32),
            pltpu.VMEM(queries.shape, jnp.bfloat16),
            pltpu.VMEM(queries.shape, jnp.bfloat16),
            pltpu.VMEM((per_core * rows, width), jnp.bfloat16),
            pltpu.VMEM((4, n_patch * rows, width), jnp.bfloat16),
            pltpu.VMEM((per_core * rows, width), jnp.bfloat16),
            pltpu.VMEM((GROUPS, rows, width), jnp.bfloat16),
            pltpu.SemaphoreType.DMA((6,)),
            pltpu.SemaphoreType.DMA((GROUPS,)),
            pltpu.SemaphoreType.DMA((4, GROUPS * n_chunk)),
            pltpu.SemaphoreType.DMA((4, n_patch // 2)),
            pltpu.SemaphoreType.DMA((per_core,)),
            pltpu.SemaphoreType.DMA((per_core,)),
            pltpu.SemaphoreType.DMA((4, n_patch)),
            pltpu.SemaphoreType.DMA((GROUPS,)),
        ],
        compiler_params=pltpu.CompilerParams(
            collective_id=0, has_side_effects=True, vmem_limit_bytes=40 * 1024 * 1024
        ),
    )(
        queries, keys, values, stale_keys, stale_values,
        q_gain.reshape(1, head_dim), k_gain.reshape(1, head_dim), o_weight,
        slot_positions.reshape(2 * n_patch, rows),
    )


def solution(mesh):
    split = P(("rep", "patch", "grp"), None)
    in_specs = (split, split, split, split, split, P(), P(), P(), P("rep"))
    return jax.shard_map(
        functools.partial(body, mesh.shape["patch"]),
        mesh=mesh, in_specs=in_specs, out_specs=split, check_vma=False,
    )
```

```python
import functools
import math

import jax
import jax.numpy as jnp
from jax import lax
from jax.experimental import pallas as pl
from jax.experimental.pallas import tpu as pltpu
from jax.sharding import PartitionSpec as P

LAT_H = 34
LAT_W = 60
GROUPS = 4
MESH = pl.DeviceIdType.MESH


def sections(head_dim):
    return (head_dim // 8, 7 * head_dim // 16, 7 * head_dim // 16)


def by_lane(lanes, head_dim, values):
    out = values[-1][2]
    for _, end, value in reversed(values[:-1]):
        out = jnp.where(lanes < end, value, out)
    return out


def rotary_tables(pos, head_dim):
    lanes = lax.broadcasted_iota(jnp.int32, (1, head_dim), 1)
    wide = lax.broadcasted_iota(jnp.int32, (head_dim, head_dim), 1)
    down = lax.broadcasted_iota(jnp.int32, (head_dim, head_dim), 0)
    line = jnp.floor((pos + 0.5) * (1.0 / LAT_W))
    col = pos - line * LAT_W
    frame = jnp.floor((line + 0.5) * (1.0 / LAT_H))
    row = line - frame * LAT_H
    at = 0
    starts, scales, signs, shifts, coords = [], [], [], [], []
    for width, coord in zip(sections(head_dim), (frame, row, col)):
        half = width // 2
        rate = -2.0 / width * math.log(256.0)
        for k in range(2):
            lo, hi = at + k * half, at + (k + 1) * half
            starts.append((lo, hi, float(lo)))
            scales.append((lo, hi, rate))
            signs.append((lo, hi, 1.0 if k else -1.0))
            shifts.append((lo, hi, -half if k else half))
        coords.append((at, at + width, coord))
        at += width
    step = lanes.astype(jnp.float32) - by_lane(lanes, head_dim, starts)
    freq = jnp.exp(step * by_lane(lanes, head_dim, scales))
    angles = by_lane(lanes, head_dim, coords) * freq
    swap = (down == wide + by_lane(wide, head_dim, shifts)).astype(jnp.float32)
    return jnp.cos(angles), jnp.sin(angles) * by_lane(lanes, head_dim, signs), swap


def row_to_column(row):
    n = row.shape[1]
    same = lax.broadcasted_iota(jnp.int32, (n, n), 0) == lax.broadcasted_iota(
        jnp.int32, (n, n), 1
    )
    return jnp.sum(jnp.where(same, row, 0.0), axis=1, keepdims=True)


def kernel(
    n_patch, heads, head_dim, rows,
    q_hbm, k_hbm, v_ref, sk_ref, sv_ref, qg_hbm, kg_hbm, w_hbm, pos_hbm,
    out_ref,
    q_ref, k_ref, qg_ref, kg_ref, w_ref, pos_ref,
    qrot, krot, qbuf, kv, osend, obuf,
    l_sem, q_ssem, kv_ssem, f_ssem, o_ssem, q_rsem, kv_rsem, o_rsem,
):
    rep = lax.axis_index("rep")
    p = lax.axis_index("patch")
    c = lax.axis_index("grp")
    hpg = heads // GROUPS
    width = hpg * head_dim
    per_group = n_patch // GROUPS
    n_chunk = per_group // 2
    chunk = n_patch // n_chunk
    per_core = chunk // 2
    my_hg = p // per_group
    my_s = p % 2
    my_qc = (p % per_group) // 2

    seq_len = 2 * n_patch * rows
    live_count = float(seq_len - max(seq_len // 256, 2))

    loads = [
        pltpu.make_async_copy(src, dst, l_sem.at[i])
        for i, (src, dst) in enumerate(
            (
                (pos_hbm, pos_ref), (qg_hbm, qg_ref), (kg_hbm, kg_ref),
                (q_hbm, q_ref), (k_hbm, k_ref), (w_hbm, w_ref),
            )
        )
    ]
    for load in loads[:5]:
        load.start()

    barrier = pltpu.get_barrier_semaphore()
    n_dev = 2 * n_patch

    def greet(i, carry):
        other = lax.rem(p * 2 + c + i, n_dev)
        pl.semaphore_signal(
            barrier, inc=1, device_id=(rep, other // 2, other % 2), device_id_type=MESH
        )
        return carry

    lax.fori_loop(1, n_dev, greet, 0)
    pl.semaphore_wait(barrier, n_dev - 1)

    pending = []

    def send(src, dst, ssem, rsem, dp, dc):
        away = jnp.logical_or(dp != p, dc != c)
        remote = pltpu.make_async_remote_copy(
            src_ref=src, dst_ref=dst, send_sem=ssem, recv_sem=rsem,
            device_id=(rep, dp, dc), device_id_type=MESH,
        )

        @pl.when(away)
        def _():
            remote.start()

        @pl.when(jnp.logical_not(away))
        def _():
            pltpu.make_async_copy(src, dst, rsem).start()

        pending.append((away, remote))

    def row_slice(i):
        return pl.ds(pl.multiple_of(i * rows, 16), rows)

    def col_slice(g):
        return pl.ds(pl.multiple_of(g * width, 128), width)

    def send_kv(kind, ref):
        stale = kind < 2
        s = (1 - c) if stale else c
        for step in range(GROUPS):
            g = lax.rem(my_hg + 1 + step, GROUPS)
            for qc in range(n_chunk):
                dp = g * per_group + qc * 2 + s
                send(
                    ref.at[:, col_slice(g)], kv.at[kind, row_slice(p), :],
                    kv_ssem.at[kind, step * n_chunk + qc], kv_rsem.at[kind, p], dp, p % 2,
                )

    def prepare(ref, gain_ref, dst):
        gain = gain_ref[...]
        a = cosine * gain
        b = sine * jnp.sum(swap * row_to_column(gain), axis=0, keepdims=True)
        for h in range(heads):
            cols = slice(h * head_dim, (h + 1) * head_dim)
            xb = ref[:, cols]
            x = xb.astype(jnp.float32)
            xs = jnp.dot(xb, swap_b, preferred_element_type=jnp.float32)
            mean_sq = jnp.mean(x * x, axis=-1, keepdims=True)
            dst[:, cols] = ((x * a + xs * b) * lax.rsqrt(mean_sq + 1e-06)).astype(jnp.bfloat16)

    send_kv(0, sk_ref)
    send_kv(1, sv_ref)
    loads[5].start()
    for load in loads[:5]:
        load.wait()
    pos = row_to_column(pos_ref[pl.ds(p * 2 + c, 1), :].astype(jnp.float32))
    cosine, sine, swap = rotary_tables(pos, head_dim)
    swap_b = swap.astype(jnp.bfloat16)
    prepare(q_ref, qg_ref, qrot)
    for step in range(GROUPS):
        g = lax.rem(my_hg + 1 + step, GROUPS)
        dp = g * per_group + (p // chunk) * 2 + c
        dc = (p % chunk) // per_core
        slot = p % per_core
        send(
            qrot.at[:, col_slice(g)], qbuf.at[row_slice(slot), :],
            q_ssem.at[step], q_rsem.at[slot], dp, dc,
        )
    prepare(k_ref, kg_ref, krot)
    send_kv(2, krot)
    send_kv(3, v_ref)

    def kv_wait(kind, src):
        piece = kv.at[kind, row_slice(src), :]
        pltpu.make_async_copy(piece, piece, kv_rsem.at[kind, src]).wait()

    def forward(kind, i):
        src = 2 * i + c
        kv_wait(kind, src)
        piece = kv.at[kind, row_slice(src), :]
        copy = pltpu.make_async_remote_copy(
            src_ref=piece, dst_ref=piece,
            send_sem=f_ssem.at[kind, i], recv_sem=kv_rsem.at[kind, src],
            device_id=(rep, p, 1 - c), device_id_type=MESH,
        )
        copy.start()
        return copy

    forwards = []
    n_q = per_core * rows
    state = [None] * hpg
    inv_root = 1.0 / head_dim**0.5
    blk = chunk * rows
    for part in range(2):
        for i in range(n_patch // 2):
            forwards.append(forward(2 * part, i))
            forwards.append(forward(2 * part + 1, i))
        if part == 0:
            for slot in range(per_core):
                piece = qbuf.at[row_slice(slot), :]
                pltpu.make_async_copy(piece, piece, q_rsem.at[slot]).wait()
        for i in range(n_patch // 2):
            kv_wait(2 * part, 2 * i + (1 - c))
            kv_wait(2 * part + 1, 2 * i + (1 - c))
        side = (1 - my_s) if part == 0 else my_s
        for at in range(0, n_patch * rows, blk):
            first = at // rows
            key_pos = jnp.concatenate(
                [pos_ref[pl.ds(2 * i + side, 1), :] for i in range(first, first + chunk)], axis=1
            )
            bias = jnp.where(key_pos.astype(jnp.float32) < live_count, 0.0, -1e30)
            for h in range(hpg):
                cols = slice(h * head_dim, (h + 1) * head_dim)
                scores = lax.dot_general(
                    qbuf[:, cols], kv[2 * part, at : at + blk, cols],
                    (((1,), (1,)), ((), ())), preferred_element_type=jnp.float32,
                )
                scores = scores * inv_root + bias
                top = jnp.max(scores, axis=1, keepdims=True)
                if state[h] is not None:
                    top = jnp.maximum(top, state[h][0])
                probs = jnp.exp(scores - top)
                total = jnp.sum(probs, axis=1, keepdims=True)
                acc = jnp.dot(
                    probs.astype(jnp.bfloat16), kv[2 * part + 1, at : at + blk, cols],
                    preferred_element_type=jnp.float32,
                )
                if state[h] is not None:
                    fade = jnp.exp(state[h][0] - top)
                    total = total + state[h][1] * fade
                    acc = acc + state[h][2] * fade
                state[h] = (top, total, acc)
    for h in range(hpg):
        cols = slice(h * head_dim, (h + 1) * head_dim)
        osend[:, cols] = (state[h][2] / state[h][1]).astype(jnp.bfloat16)
    for slot in range(per_core):
        dp = my_qc * chunk + c * per_core + slot
        send(
            osend.at[row_slice(slot), :], obuf.at[my_hg],
            o_ssem.at[slot], o_rsem.at[my_hg], dp, my_s,
        )
    for g in range(GROUPS):
        piece = obuf.at[g]
        pltpu.make_async_copy(piece, piece, o_rsem.at[g]).wait()
    attn = jnp.concatenate([obuf[g] for g in range(GROUPS)], axis=1)
    loads[5].wait()
    own_live = pos < live_count
    d_out = out_ref.shape[1]
    for at in range(0, d_out, 512):
        tile = jnp.dot(attn, w_ref[:, at : at + 512], preferred_element_type=jnp.float32)
        out_ref[:, at : at + 512] = jnp.where(own_live, tile, 0.0).astype(jnp.bfloat16)
    for copy in forwards:
        copy.wait_send()
    for away, remote in pending:

        @pl.when(away)
        def _():
            remote.wait_send()


def body(n_patch, queries, keys, values, stale_keys, stale_values, q_gain, k_gain, o_weight, slot_positions):
    rows = queries.shape[0]
    head_dim = q_gain.shape[0]
    heads = queries.shape[1] // head_dim
    width = heads // GROUPS * head_dim
    n_chunk = n_patch // GROUPS // 2
    per_core = n_patch // n_chunk // 2
    hbm = pl.BlockSpec(memory_space=pltpu.HBM)
    return pl.pallas_call(
        functools.partial(kernel, n_patch, heads, head_dim, rows),
        out_shape=jax.ShapeDtypeStruct((rows, o_weight.shape[1]), jnp.bfloat16),
        in_specs=[hbm] * 9,
        out_specs=pl.BlockSpec(memory_space=pltpu.VMEM),
        scratch_shapes=[
            pltpu.VMEM(queries.shape, jnp.bfloat16),
            pltpu.VMEM(queries.shape, jnp.bfloat16),
            pltpu.VMEM((1, head_dim), jnp.float32),
            pltpu.VMEM((1, head_dim), jnp.float32),
            pltpu.VMEM(o_weight.shape, jnp.bfloat16),
            pltpu.VMEM((2 * n_patch, rows), jnp.int32),
            pltpu.VMEM(queries.shape, jnp.bfloat16),
            pltpu.VMEM(queries.shape, jnp.bfloat16),
            pltpu.VMEM((per_core * rows, width), jnp.bfloat16),
            pltpu.VMEM((4, n_patch * rows, width), jnp.bfloat16),
            pltpu.VMEM((per_core * rows, width), jnp.bfloat16),
            pltpu.VMEM((GROUPS, rows, width), jnp.bfloat16),
            pltpu.SemaphoreType.DMA((6,)),
            pltpu.SemaphoreType.DMA((GROUPS,)),
            pltpu.SemaphoreType.DMA((4, GROUPS * n_chunk)),
            pltpu.SemaphoreType.DMA((4, n_patch // 2)),
            pltpu.SemaphoreType.DMA((per_core,)),
            pltpu.SemaphoreType.DMA((per_core,)),
            pltpu.SemaphoreType.DMA((4, n_patch)),
            pltpu.SemaphoreType.DMA((GROUPS,)),
        ],
        compiler_params=pltpu.CompilerParams(
            collective_id=0, has_side_effects=True, vmem_limit_bytes=60 * 1024 * 1024
        ),
    )(
        queries, keys, values, stale_keys, stale_values,
        q_gain.reshape(1, head_dim), k_gain.reshape(1, head_dim), o_weight,
        slot_positions.reshape(2 * n_patch, rows),
    )


def solution(mesh):
    split = P(("rep", "patch", "grp"), None)
    in_specs = (split, split, split, split, split, P(), P(), P(), P("rep"))
    return jax.shard_map(
        functools.partial(body, mesh.shape["patch"]),
        mesh=mesh, in_specs=in_specs, out_specs=split, check_vma=False,
    )
```

```python
import functools
import math

import jax
import jax.numpy as jnp
from jax import lax
from jax.experimental import pallas as pl
from jax.experimental.pallas import tpu as pltpu
from jax.sharding import PartitionSpec as P

LAT_H = 34
LAT_W = 60
GROUPS = 4
MESH = pl.DeviceIdType.MESH


def sections(head_dim):
    return (head_dim // 8, 7 * head_dim // 16, 7 * head_dim // 16)


def by_lane(lanes, head_dim, values):
    out = values[-1][2]
    for _, end, value in reversed(values[:-1]):
        out = jnp.where(lanes < end, value, out)
    return out


def rotary_tables(pos, head_dim):
    lanes = lax.broadcasted_iota(jnp.int32, (1, head_dim), 1)
    wide = lax.broadcasted_iota(jnp.int32, (head_dim, head_dim), 1)
    down = lax.broadcasted_iota(jnp.int32, (head_dim, head_dim), 0)
    line = jnp.floor((pos + 0.5) * (1.0 / LAT_W))
    col = pos - line * LAT_W
    frame = jnp.floor((line + 0.5) * (1.0 / LAT_H))
    row = line - frame * LAT_H
    at = 0
    starts, scales, signs, shifts, coords = [], [], [], [], []
    for width, coord in zip(sections(head_dim), (frame, row, col)):
        half = width // 2
        rate = -2.0 / width * math.log(256.0)
        for k in range(2):
            lo, hi = at + k * half, at + (k + 1) * half
            starts.append((lo, hi, float(lo)))
            scales.append((lo, hi, rate))
            signs.append((lo, hi, 1.0 if k else -1.0))
            shifts.append((lo, hi, -half if k else half))
        coords.append((at, at + width, coord))
        at += width
    step = lanes.astype(jnp.float32) - by_lane(lanes, head_dim, starts)
    freq = jnp.exp(step * by_lane(lanes, head_dim, scales))
    angles = by_lane(lanes, head_dim, coords) * freq
    swap = (down == wide + by_lane(wide, head_dim, shifts)).astype(jnp.float32)
    return jnp.cos(angles), jnp.sin(angles) * by_lane(lanes, head_dim, signs), swap


def row_to_column(row):
    n = row.shape[1]
    same = lax.broadcasted_iota(jnp.int32, (n, n), 0) == lax.broadcasted_iota(
        jnp.int32, (n, n), 1
    )
    return jnp.sum(jnp.where(same, row, 0.0), axis=1, keepdims=True)


def kernel(
    n_patch, heads, head_dim, rows,
    q_hbm, k_hbm, v_ref, sk_ref, sv_ref, qg_hbm, kg_hbm, w_hbm, pos_hbm,
    out_ref,
    q_ref, k_ref, qg_ref, kg_ref, w_ref, pos_ref,
    qrot, krot, qbuf, kv, osend, obuf,
    l_sem, q_ssem, kv_ssem, f_ssem, o_ssem, q_rsem, kv_rsem, o_rsem,
):
    rep = lax.axis_index("rep")
    p = lax.axis_index("patch")
    c = lax.axis_index("grp")
    hpg = heads // GROUPS
    width = hpg * head_dim
    per_group = n_patch // GROUPS
    n_chunk = per_group // 2
    chunk = n_patch // n_chunk
    per_core = chunk // 2
    my_hg = p // per_group
    my_s = p % 2
    my_qc = (p % per_group) // 2

    seq_len = 2 * n_patch * rows
    live_count = float(seq_len - max(seq_len // 256, 2))

    loads = [
        pltpu.make_async_copy(src, dst, l_sem.at[i])
        for i, (src, dst) in enumerate(
            (
                (pos_hbm, pos_ref), (qg_hbm, qg_ref), (kg_hbm, kg_ref),
                (q_hbm, q_ref), (k_hbm, k_ref), (w_hbm, w_ref),
            )
        )
    ]
    for load in loads[:5]:
        load.start()

    barrier = pltpu.get_barrier_semaphore()
    n_dev = 2 * n_patch

    def greet(i, carry):
        other = lax.rem(p * 2 + c + i, n_dev)
        pl.semaphore_signal(
            barrier, inc=1, device_id=(rep, other // 2, other % 2), device_id_type=MESH
        )
        return carry

    lax.fori_loop(1, n_dev, greet, 0)
    pl.semaphore_wait(barrier, n_dev - 1)

    pending = []

    def send(src, dst, ssem, rsem, dp, dc):
        away = jnp.logical_or(dp != p, dc != c)
        remote = pltpu.make_async_remote_copy(
            src_ref=src, dst_ref=dst, send_sem=ssem, recv_sem=rsem,
            device_id=(rep, dp, dc), device_id_type=MESH,
        )

        @pl.when(away)
        def _():
            remote.start()

        @pl.when(jnp.logical_not(away))
        def _():
            pltpu.make_async_copy(src, dst, rsem).start()

        pending.append((away, remote))

    def row_slice(i):
        return pl.ds(pl.multiple_of(i * rows, 16), rows)

    def col_slice(g):
        return pl.ds(pl.multiple_of(g * width, 128), width)

    def send_kv(kind, ref):
        stale = kind < 2
        s = (1 - c) if stale else c
        for step in range(GROUPS):
            g = lax.rem(my_hg + 1 + step, GROUPS)
            for qc in range(n_chunk):
                dp = g * per_group + qc * 2 + s
                send(
                    ref.at[:, col_slice(g)], kv.at[kind, row_slice(p), :],
                    kv_ssem.at[kind, step * n_chunk + qc], kv_rsem.at[kind, p], dp, p % 2,
                )

    def prepare(ref, gain_ref, dst):
        gain = gain_ref[...]
        a = cosine * gain
        b = sine * jnp.sum(swap * row_to_column(gain), axis=0, keepdims=True)
        for h in range(heads):
            cols = slice(h * head_dim, (h + 1) * head_dim)
            xb = ref[:, cols]
            x = xb.astype(jnp.float32)
            xs = jnp.dot(xb, swap_b, preferred_element_type=jnp.float32)
            mean_sq = jnp.mean(x * x, axis=-1, keepdims=True)
            dst[:, cols] = ((x * a + xs * b) * lax.rsqrt(mean_sq + 1e-06)).astype(jnp.bfloat16)

    send_kv(0, sk_ref)
    send_kv(1, sv_ref)
    loads[5].start()
    for load in loads[:5]:
        load.wait()
    all_pos = pos_ref[...].reshape(1, seq_len).astype(jnp.float32)
    here = lax.broadcasted_iota(jnp.int32, (rows, seq_len), 1) == (
        lax.broadcasted_iota(jnp.int32, (rows, seq_len), 0) + (p * 2 + c) * rows
    )
    pos = jnp.sum(jnp.where(here, all_pos, 0.0), axis=1, keepdims=True)
    cosine, sine, swap = rotary_tables(pos, head_dim)
    swap_b = swap.astype(jnp.bfloat16)
    prepare(q_ref, qg_ref, qrot)
    for step in range(GROUPS):
        g = lax.rem(my_hg + 1 + step, GROUPS)
        dp = g * per_group + (p // chunk) * 2 + c
        dc = (p % chunk) // per_core
        slot = p % per_core
        send(
            qrot.at[:, col_slice(g)], qbuf.at[row_slice(slot), :],
            q_ssem.at[step], q_rsem.at[slot], dp, dc,
        )
    prepare(k_ref, kg_ref, krot)
    send_kv(2, krot)
    send_kv(3, v_ref)

    def kv_wait(kind, src):
        piece = kv.at[kind, row_slice(src), :]
        pltpu.make_async_copy(piece, piece, kv_rsem.at[kind, src]).wait()

    def forward(kind, i):
        src = 2 * i + c
        kv_wait(kind, src)
        piece = kv.at[kind, row_slice(src), :]
        copy = pltpu.make_async_remote_copy(
            src_ref=piece, dst_ref=piece,
            send_sem=f_ssem.at[kind, i], recv_sem=kv_rsem.at[kind, src],
            device_id=(rep, p, 1 - c), device_id_type=MESH,
        )
        copy.start()
        return copy

    forwards = []
    n_q = per_core * rows
    state = [None] * hpg
    inv_root = 1.0 / head_dim**0.5
    blk = chunk * rows
    for part in range(2):
        for i in range(n_patch // 2):
            forwards.append(forward(2 * part, i))
            forwards.append(forward(2 * part + 1, i))
        if part == 0:
            for slot in range(per_core):
                piece = qbuf.at[row_slice(slot), :]
                pltpu.make_async_copy(piece, piece, q_rsem.at[slot]).wait()
        for i in range(n_patch // 2):
            kv_wait(2 * part, 2 * i + (1 - c))
            kv_wait(2 * part + 1, 2 * i + (1 - c))
        side = (1 - my_s) if part == 0 else my_s
        for at in range(0, n_patch * rows, blk):
            first = at // rows
            even, odd = (
                jnp.concatenate(
                    [
                        all_pos[:, (2 * i + k) * rows : (2 * i + k + 1) * rows]
                        for i in range(first, first + chunk)
                    ],
                    axis=1,
                )
                for k in range(2)
            )
            key_pos = jnp.where(side == 0, even, odd)
            bias = jnp.where(key_pos < live_count, 0.0, -1e30)
            for h in range(hpg):
                cols = slice(h * head_dim, (h + 1) * head_dim)
                scores = lax.dot_general(
                    qbuf[:, cols], kv[2 * part, at : at + blk, cols],
                    (((1,), (1,)), ((), ())), preferred_element_type=jnp.float32,
                )
                scores = scores * inv_root + bias
                top = jnp.max(scores, axis=1, keepdims=True)
                if state[h] is not None:
                    top = jnp.maximum(top, state[h][0])
                probs = jnp.exp(scores - top)
                total = jnp.sum(probs, axis=1, keepdims=True)
                acc = jnp.dot(
                    probs.astype(jnp.bfloat16), kv[2 * part + 1, at : at + blk, cols],
                    preferred_element_type=jnp.float32,
                )
                if state[h] is not None:
                    fade = jnp.exp(state[h][0] - top)
                    total = total + state[h][1] * fade
                    acc = acc + state[h][2] * fade
                state[h] = (top, total, acc)
    for h in range(hpg):
        cols = slice(h * head_dim, (h + 1) * head_dim)
        osend[:, cols] = (state[h][2] / state[h][1]).astype(jnp.bfloat16)
    for slot in range(per_core):
        dp = my_qc * chunk + c * per_core + slot
        send(
            osend.at[row_slice(slot), :], obuf.at[my_hg],
            o_ssem.at[slot], o_rsem.at[my_hg], dp, my_s,
        )
    for g in range(GROUPS):
        piece = obuf.at[g]
        pltpu.make_async_copy(piece, piece, o_rsem.at[g]).wait()
    attn = jnp.concatenate([obuf[g] for g in range(GROUPS)], axis=1)
    loads[5].wait()
    own_live = pos < live_count
    d_out = out_ref.shape[1]
    for at in range(0, d_out, 512):
        tile = jnp.dot(attn, w_ref[:, at : at + 512], preferred_element_type=jnp.float32)
        out_ref[:, at : at + 512] = jnp.where(own_live, tile, 0.0).astype(jnp.bfloat16)
    for copy in forwards:
        copy.wait_send()
    for away, remote in pending:

        @pl.when(away)
        def _():
            remote.wait_send()


def body(n_patch, queries, keys, values, stale_keys, stale_values, q_gain, k_gain, o_weight, slot_positions):
    rows = queries.shape[0]
    head_dim = q_gain.shape[0]
    heads = queries.shape[1] // head_dim
    width = heads // GROUPS * head_dim
    n_chunk = n_patch // GROUPS // 2
    per_core = n_patch // n_chunk // 2
    hbm = pl.BlockSpec(memory_space=pltpu.HBM)
    return pl.pallas_call(
        functools.partial(kernel, n_patch, heads, head_dim, rows),
        out_shape=jax.ShapeDtypeStruct((rows, o_weight.shape[1]), jnp.bfloat16),
        in_specs=[hbm] * 9,
        out_specs=pl.BlockSpec(memory_space=pltpu.VMEM),
        scratch_shapes=[
            pltpu.VMEM(queries.shape, jnp.bfloat16),
            pltpu.VMEM(queries.shape, jnp.bfloat16),
            pltpu.VMEM((1, head_dim), jnp.float32),
            pltpu.VMEM((1, head_dim), jnp.float32),
            pltpu.VMEM(o_weight.shape, jnp.bfloat16),
            pltpu.VMEM((2 * n_patch * rows,), jnp.int32),
            pltpu.VMEM(queries.shape, jnp.bfloat16),
            pltpu.VMEM(queries.shape, jnp.bfloat16),
            pltpu.VMEM((per_core * rows, width), jnp.bfloat16),
            pltpu.VMEM((4, n_patch * rows, width), jnp.bfloat16),
            pltpu.VMEM((per_core * rows, width), jnp.bfloat16),
            pltpu.VMEM((GROUPS, rows, width), jnp.bfloat16),
            pltpu.SemaphoreType.DMA((6,)),
            pltpu.SemaphoreType.DMA((GROUPS,)),
            pltpu.SemaphoreType.DMA((4, GROUPS * n_chunk)),
            pltpu.SemaphoreType.DMA((4, n_patch // 2)),
            pltpu.SemaphoreType.DMA((per_core,)),
            pltpu.SemaphoreType.DMA((per_core,)),
            pltpu.SemaphoreType.DMA((4, n_patch)),
            pltpu.SemaphoreType.DMA((GROUPS,)),
        ],
        compiler_params=pltpu.CompilerParams(
            collective_id=0, has_side_effects=True, vmem_limit_bytes=60 * 1024 * 1024
        ),
    )(
        queries, keys, values, stale_keys, stale_values,
        q_gain.reshape(1, head_dim), k_gain.reshape(1, head_dim), o_weight,
        slot_positions,
    )


def solution(mesh):
    split = P(("rep", "patch", "grp"), None)
    in_specs = (split, split, split, split, split, P(), P(), P(), P("rep"))
    return jax.shard_map(
        functools.partial(body, mesh.shape["patch"]),
        mesh=mesh, in_specs=in_specs, out_specs=split, check_vma=False,
    )
```

```python
import functools
import math

import jax
import jax.numpy as jnp
from jax import lax
from jax.experimental import pallas as pl
from jax.experimental.pallas import tpu as pltpu
from jax.sharding import PartitionSpec as P

LAT_H = 34
LAT_W = 60
GROUPS = 4
MESH = pl.DeviceIdType.MESH


def sections(head_dim):
    return (head_dim // 8, 7 * head_dim // 16, 7 * head_dim // 16)


def by_lane(lanes, head_dim, values):
    out = values[-1][2]
    for _, end, value in reversed(values[:-1]):
        out = jnp.where(lanes < end, value, out)
    return out


def rotary_tables(pos, head_dim):
    lanes = lax.broadcasted_iota(jnp.int32, (1, head_dim), 1)
    wide = lax.broadcasted_iota(jnp.int32, (head_dim, head_dim), 1)
    down = lax.broadcasted_iota(jnp.int32, (head_dim, head_dim), 0)
    line = jnp.floor((pos + 0.5) * (1.0 / LAT_W))
    col = pos - line * LAT_W
    frame = jnp.floor((line + 0.5) * (1.0 / LAT_H))
    row = line - frame * LAT_H
    at = 0
    starts, scales, signs, shifts, coords = [], [], [], [], []
    for width, coord in zip(sections(head_dim), (frame, row, col)):
        half = width // 2
        rate = -2.0 / width * math.log(256.0)
        for k in range(2):
            lo, hi = at + k * half, at + (k + 1) * half
            starts.append((lo, hi, float(lo)))
            scales.append((lo, hi, rate))
            signs.append((lo, hi, 1.0 if k else -1.0))
            shifts.append((lo, hi, -half if k else half))
        coords.append((at, at + width, coord))
        at += width
    step = lanes.astype(jnp.float32) - by_lane(lanes, head_dim, starts)
    freq = jnp.exp(step * by_lane(lanes, head_dim, scales))
    angles = by_lane(lanes, head_dim, coords) * freq
    swap = (down == wide + by_lane(wide, head_dim, shifts)).astype(jnp.float32)
    return jnp.cos(angles), jnp.sin(angles) * by_lane(lanes, head_dim, signs), swap


def row_to_column(row):
    n = row.shape[1]
    same = lax.broadcasted_iota(jnp.int32, (n, n), 0) == lax.broadcasted_iota(
        jnp.int32, (n, n), 1
    )
    return jnp.sum(jnp.where(same, row, 0.0), axis=1, keepdims=True)


def kernel(
    n_patch, heads, head_dim, rows,
    q_hbm, k_hbm, v_ref, sk_ref, sv_ref, qg_hbm, kg_hbm, w_hbm, pos_hbm,
    out_ref,
    q_ref, k_ref, qg_ref, kg_ref, w_ref, pos_ref,
    qrot, krot, qbuf, kv, osend, obuf, proj,
    l_sem, q_ssem, kv_ssem, f_ssem, o_ssem, q_rsem, kv_rsem, o_rsem,
):
    rep = lax.axis_index("rep")
    p = lax.axis_index("patch")
    c = lax.axis_index("grp")
    hpg = heads // GROUPS
    width = hpg * head_dim
    per_group = n_patch // GROUPS
    n_chunk = per_group // 2
    chunk = n_patch // n_chunk
    per_core = chunk // 2
    my_hg = p // per_group
    my_s = p % 2
    my_qc = (p % per_group) // 2

    seq_len = 2 * n_patch * rows
    live_count = float(seq_len - max(seq_len // 256, 2))

    loads = [
        pltpu.make_async_copy(src, dst, l_sem.at[i])
        for i, (src, dst) in enumerate(
            (
                (pos_hbm, pos_ref), (qg_hbm, qg_ref), (kg_hbm, kg_ref),
                (q_hbm, q_ref), (k_hbm, k_ref), (w_hbm, w_ref),
            )
        )
    ]
    for load in loads[:5]:
        load.start()

    barrier = pltpu.get_barrier_semaphore()
    n_dev = 2 * n_patch

    def greet(i, carry):
        other = lax.rem(p * 2 + c + i, n_dev)
        pl.semaphore_signal(
            barrier, inc=1, device_id=(rep, other // 2, other % 2), device_id_type=MESH
        )
        return carry

    lax.fori_loop(1, n_dev, greet, 0)
    pl.semaphore_wait(barrier, n_dev - 1)

    pending = []

    def send(src, dst, ssem, rsem, dp, dc):
        away = jnp.logical_or(dp != p, dc != c)
        remote = pltpu.make_async_remote_copy(
            src_ref=src, dst_ref=dst, send_sem=ssem, recv_sem=rsem,
            device_id=(rep, dp, dc), device_id_type=MESH,
        )

        @pl.when(away)
        def _():
            remote.start()

        @pl.when(jnp.logical_not(away))
        def _():
            pltpu.make_async_copy(src, dst, rsem).start()

        pending.append((away, remote))

    def row_slice(i):
        return pl.ds(pl.multiple_of(i * rows, 16), rows)

    def col_slice(g):
        return pl.ds(pl.multiple_of(g * width, 128), width)

    def send_kv(kind, ref):
        stale = kind < 2
        s = (1 - c) if stale else c
        for step in range(GROUPS):
            g = lax.rem(my_hg + 1 + step, GROUPS)
            for qc in range(n_chunk):
                dp = g * per_group + qc * 2 + s
                send(
                    ref.at[:, col_slice(g)], kv.at[kind, row_slice(p), :],
                    kv_ssem.at[kind, step * n_chunk + qc], kv_rsem.at[kind, p], dp, p % 2,
                )

    def prepare(ref, gain_ref, dst):
        gain = gain_ref[...]
        a = cosine * gain
        b = sine * jnp.sum(swap * row_to_column(gain), axis=0, keepdims=True)
        for h in range(heads):
            cols = slice(h * head_dim, (h + 1) * head_dim)
            xb = ref[:, cols]
            x = xb.astype(jnp.float32)
            xs = jnp.dot(xb, swap_b, preferred_element_type=jnp.float32)
            mean_sq = jnp.mean(x * x, axis=-1, keepdims=True)
            dst[:, cols] = ((x * a + xs * b) * lax.rsqrt(mean_sq + 1e-06)).astype(jnp.bfloat16)

    send_kv(0, sk_ref)
    send_kv(1, sv_ref)
    loads[5].start()
    for load in loads[:5]:
        load.wait()
    all_pos = pos_ref[...].reshape(1, seq_len).astype(jnp.float32)
    here = lax.broadcasted_iota(jnp.int32, (rows, seq_len), 1) == (
        lax.broadcasted_iota(jnp.int32, (rows, seq_len), 0) + (p * 2 + c) * rows
    )
    pos = jnp.sum(jnp.where(here, all_pos, 0.0), axis=1, keepdims=True)
    cosine, sine, swap = rotary_tables(pos, head_dim)
    swap_b = swap.astype(jnp.bfloat16)
    prepare(q_ref, qg_ref, qrot)
    for step in range(GROUPS):
        g = lax.rem(my_hg + 1 + step, GROUPS)
        dp = g * per_group + (p // chunk) * 2 + c
        dc = (p % chunk) // per_core
        slot = p % per_core
        send(
            qrot.at[:, col_slice(g)], qbuf.at[row_slice(slot), :],
            q_ssem.at[step], q_rsem.at[slot], dp, dc,
        )
    prepare(k_ref, kg_ref, krot)
    send_kv(2, krot)
    send_kv(3, v_ref)

    def kv_wait(kind, src):
        piece = kv.at[kind, row_slice(src), :]
        pltpu.make_async_copy(piece, piece, kv_rsem.at[kind, src]).wait()

    def forward(kind, i):
        src = 2 * i + c
        kv_wait(kind, src)
        piece = kv.at[kind, row_slice(src), :]
        copy = pltpu.make_async_remote_copy(
            src_ref=piece, dst_ref=piece,
            send_sem=f_ssem.at[kind, i], recv_sem=kv_rsem.at[kind, src],
            device_id=(rep, p, 1 - c), device_id_type=MESH,
        )
        copy.start()
        return copy

    forwards = []
    n_q = per_core * rows
    state = [None] * hpg
    inv_root = 1.0 / head_dim**0.5
    blk = chunk * rows
    for part in range(2):
        for i in range(n_patch // 2):
            forwards.append(forward(2 * part, i))
            forwards.append(forward(2 * part + 1, i))
        if part == 0:
            for slot in range(per_core):
                piece = qbuf.at[row_slice(slot), :]
                pltpu.make_async_copy(piece, piece, q_rsem.at[slot]).wait()
        for i in range(n_patch // 2):
            kv_wait(2 * part, 2 * i + (1 - c))
            kv_wait(2 * part + 1, 2 * i + (1 - c))
        side = (1 - my_s) if part == 0 else my_s
        for at in range(0, n_patch * rows, blk):
            first = at // rows
            even, odd = (
                jnp.concatenate(
                    [
                        all_pos[:, (2 * i + k) * rows : (2 * i + k + 1) * rows]
                        for i in range(first, first + chunk)
                    ],
                    axis=1,
                )
                for k in range(2)
            )
            key_pos = jnp.where(side == 0, even, odd)
            bias = jnp.where(key_pos < live_count, 0.0, -1e30)
            for h in range(hpg):
                cols = slice(h * head_dim, (h + 1) * head_dim)
                scores = lax.dot_general(
                    qbuf[:, cols], kv[2 * part, at : at + blk, cols],
                    (((1,), (1,)), ((), ())), preferred_element_type=jnp.float32,
                )
                scores = scores * inv_root + bias
                top = jnp.max(scores, axis=1, keepdims=True)
                if state[h] is not None:
                    top = jnp.maximum(top, state[h][0])
                probs = jnp.exp(scores - top)
                total = jnp.sum(probs, axis=1, keepdims=True)
                acc = jnp.dot(
                    probs.astype(jnp.bfloat16), kv[2 * part + 1, at : at + blk, cols],
                    preferred_element_type=jnp.float32,
                )
                if state[h] is not None:
                    fade = jnp.exp(state[h][0] - top)
                    total = total + state[h][1] * fade
                    acc = acc + state[h][2] * fade
                state[h] = (top, total, acc)
    for h in range(hpg):
        cols = slice(h * head_dim, (h + 1) * head_dim)
        osend[:, cols] = (state[h][2] / state[h][1]).astype(jnp.bfloat16)
    for slot in range(per_core):
        dp = my_qc * chunk + c * per_core + slot
        send(
            osend.at[row_slice(slot), :], obuf.at[my_hg],
            o_ssem.at[slot], o_rsem.at[my_hg], dp, my_s,
        )
    loads[5].wait()
    own_live = pos < live_count
    d_out = out_ref.shape[1]
    turn = 1 - 2 * (my_hg // (GROUPS // 2))
    for step in range(GROUPS):
        g = lax.rem(my_hg + step * turn + GROUPS, GROUPS)
        piece = obuf.at[g]
        pltpu.make_async_copy(piece, piece, o_rsem.at[g]).wait()
        attn = obuf[g]
        for at in range(0, d_out, 512):
            tile = jnp.dot(
                attn, w_ref[col_slice(g), at : at + 512], preferred_element_type=jnp.float32
            )
            if step > 0:
                tile = tile + proj[:, at : at + 512]
            if step < GROUPS - 1:
                proj[:, at : at + 512] = tile
            else:
                out_ref[:, at : at + 512] = jnp.where(own_live, tile, 0.0).astype(jnp.bfloat16)
    for copy in forwards:
        copy.wait_send()
    for away, remote in pending:

        @pl.when(away)
        def _():
            remote.wait_send()


def body(n_patch, queries, keys, values, stale_keys, stale_values, q_gain, k_gain, o_weight, slot_positions):
    rows = queries.shape[0]
    head_dim = q_gain.shape[0]
    heads = queries.shape[1] // head_dim
    width = heads // GROUPS * head_dim
    n_chunk = n_patch // GROUPS // 2
    per_core = n_patch // n_chunk // 2
    hbm = pl.BlockSpec(memory_space=pltpu.HBM)
    return pl.pallas_call(
        functools.partial(kernel, n_patch, heads, head_dim, rows),
        out_shape=jax.ShapeDtypeStruct((rows, o_weight.shape[1]), jnp.bfloat16),
        in_specs=[hbm] * 9,
        out_specs=pl.BlockSpec(memory_space=pltpu.VMEM),
        scratch_shapes=[
            pltpu.VMEM(queries.shape, jnp.bfloat16),
            pltpu.VMEM(queries.shape, jnp.bfloat16),
            pltpu.VMEM((1, head_dim), jnp.float32),
            pltpu.VMEM((1, head_dim), jnp.float32),
            pltpu.VMEM(o_weight.shape, jnp.bfloat16),
            pltpu.VMEM((2 * n_patch * rows,), jnp.int32),
            pltpu.VMEM(queries.shape, jnp.bfloat16),
            pltpu.VMEM(queries.shape, jnp.bfloat16),
            pltpu.VMEM((per_core * rows, width), jnp.bfloat16),
            pltpu.VMEM((4, n_patch * rows, width), jnp.bfloat16),
            pltpu.VMEM((per_core * rows, width), jnp.bfloat16),
            pltpu.VMEM((GROUPS, rows, width), jnp.bfloat16),
            pltpu.VMEM((rows, o_weight.shape[1]), jnp.float32),
            pltpu.SemaphoreType.DMA((6,)),
            pltpu.SemaphoreType.DMA((GROUPS,)),
            pltpu.SemaphoreType.DMA((4, GROUPS * n_chunk)),
            pltpu.SemaphoreType.DMA((4, n_patch // 2)),
            pltpu.SemaphoreType.DMA((per_core,)),
            pltpu.SemaphoreType.DMA((per_core,)),
            pltpu.SemaphoreType.DMA((4, n_patch)),
            pltpu.SemaphoreType.DMA((GROUPS,)),
        ],
        compiler_params=pltpu.CompilerParams(
            collective_id=0, has_side_effects=True, vmem_limit_bytes=60 * 1024 * 1024
        ),
    )(
        queries, keys, values, stale_keys, stale_values,
        q_gain.reshape(1, head_dim), k_gain.reshape(1, head_dim), o_weight,
        slot_positions,
    )


def solution(mesh):
    split = P(("rep", "patch", "grp"), None)
    in_specs = (split, split, split, split, split, P(), P(), P(), P("rep"))
    return jax.shard_map(
        functools.partial(body, mesh.shape["patch"]),
        mesh=mesh, in_specs=in_specs, out_specs=split, check_vma=False,
    )
```
